1024 devices in a mesh: row: 32 (over x, z_lo, core), col: 8 (over y), layer: 4 (over z_hi).
Axes of the slice: x: 4, y: 8, z: 16 (z_hi: 4, z_lo: 4; z = z_hi * 4 + z_lo), core: 2. Of those that a mesh axis runs over, the one named last changes fastest.
Arguments:
- x_blocks: bfloat16 [2048, 32, 1024], P('row', None, 'col'), may hold values from -1.5 to 1.5
- shifts: int32 [32, 32], replicated, may hold values from 0 to 63
Outputs:
- squared: bfloat16 [2048, 32, 1024], P(('row', 'layer'), None, 'col')
The draws below stay inside these ranges and needn't reach their ends.
All inputs are finite; a program needn't handle non-finite values.
Results may differ from the reference program's by a relative error of at most 0.001.
Values may be sent and summed in bfloat16 or wider, within the bound.
No kernel may reach another device: no remote copies, remote signals or barrier semaphores. Data moves between devices by JAX's collectives and lax.ppermute only.
A program may use at most 32 MiB of HBM per device.

```python
import jax
import jax.numpy as jnp
from jax import lax

BS = 32
NB = 2048
NR = 32
RANGE = 64


def draw_shifts(key, part):
    key_base = jax.random.fold_in(key, 11)
    key_noise = jax.random.fold_in(key, 23)
    base = jax.random.randint(key_base, (NR,), 0, RANGE)
    noise = jax.random.randint(key_noise, (NR, NR), -1, 2)
    return ((base[None, :] - base[:, None] + noise) % RANGE).astype(jnp.int32)


def shard_levels(key, shape, pieces, smallest, top_value):
    gain, own = 1.0, jax.random.fold_in(key, 6)
    for position, blocks in pieces:
        heights = jnp.exp(jax.random.uniform(jax.random.fold_in(own, position), (blocks,), jnp.float32, smallest / len(pieces), top_value / len(pieces)))
        gain = gain * jnp.repeat(heights, shape[position] // blocks).reshape([-1 if axis == position else 1 for axis in range(len(shape))])
    return gain


def scatter_about(key, dims, spread, most, cuts=(), kind=jnp.bfloat16):
    entries = jax.random.normal(key, dims, jnp.float32) * spread
    if len(cuts) > 0:
        entries = shard_levels(key, dims, cuts, -0.22, 0.18) * entries
    return jnp.clip(entries, min=-most, max=most).astype(kind)


def setup_inputs(seed: int = 0) -> dict:
    streams_of = jax.random.split(jax.random.key(seed), 3)
    x_blocks = scatter_about(streams_of[0], (NB, BS, NR * BS), 0.25, 1.5, ((0, 32), (2, 8)))
    shifts = draw_shifts(jax.random.fold_in(streams_of[2], 71), 0)
    return dict(x_blocks=x_blocks, shifts=shifts)


def range_product(x_wide, shifts, target):
    rows_here = lax.dynamic_slice_in_dim(x_wide, target * RANGE, RANGE, 0)

    def add_range(source, totals):
        source_index = jnp.asarray(source).astype(jnp.int32)
        left_blocks = lax.dynamic_slice_in_dim(rows_here, source_index * BS, BS, 2)
        right_rows = lax.dynamic_slice_in_dim(x_wide, source_index * RANGE, RANGE, 0)
        doubled = jnp.concatenate([right_rows, right_rows], axis=0)
        offset_here = shifts[target, source_index]
        right_blocks = lax.dynamic_slice_in_dim(doubled, offset_here, RANGE, 0)
        matches = (offset_here + shifts[source_index] - shifts[target]) % RANGE == 0
        column_mask = jnp.repeat(matches, BS)
        product_terms = jnp.einsum("pij,pjk->pik", left_blocks, right_blocks)
        return totals + jnp.where(column_mask[None, None, :], product_terms, 0.0)

    empty_sum = jnp.zeros((RANGE, BS, NR * BS), x_wide.dtype)
    return lax.fori_loop(0, NR, add_range, empty_sum)


def reference(x_blocks, shifts):
    x_wide = x_blocks.astype(jnp.float32)
    targets = jnp.arange(NR, dtype=jnp.int32)
    blocks = lax.map(lambda target: range_product(x_wide, shifts, target), targets)
    return blocks.reshape(NB, BS, NR * BS).astype(jnp.bfloat16)
```

```python
import jax
import jax.numpy as jnp
from jax import lax
from jax.experimental import pallas as pl
from jax.experimental.pallas import tpu as pltpu
from jax.sharding import PartitionSpec as P

AXES = ("row", "col", "layer")
NX, NZ, NY, NL = 4, 4, 8, 4
BS, RANGE, SPAN = 32, 64, 16
LANES = 128
NEAR = 8
STEPS = (0, 1, -1, 2)


def device_pairs(move):
    def index(x, z, core, y):
        return ((x * NZ + z % NZ) * 2 + core) * NY * NL + y * NL + z // NZ

    pairs = []
    for x in range(NX):
        for z in range(NZ * NL):
            for core in range(2):
                for y in range(NY):
                    tx, tz, tcore, ty = move(x, z, core, y)
                    pairs.append((index(x, z, core, y), index(tx % NX, tz % (NZ * NL), tcore, ty % NY)))
    return pairs


def sent(value, move):
    return lax.ppermute(value, AXES, device_pairs(move))


def other_core(x, z, core, y):
    return x, z, 1 - core, y


def along_x(step):
    return lambda x, z, core, y: (x + step, z, core, y)


def along_z(step):
    return lambda x, z, core, y: (x, z + step, core, y)


def two_along_z(x, z, core, y):
    return x, (z + 2 if core == 0 else z - 2), core, y


def target_row(row, step):
    return (((row >> 3) - step) & (NX - 1)) * NEAR + (row & (NEAR - 1))


def mask_kernel(place_ref, shifts_ref, masks_ref):
    row = place_ref[0]
    col = place_ref[1]
    near = (row >> 3) * NEAR
    lane_block = lax.broadcasted_iota(jnp.int32, (BS, LANES), 1) // BS

    def mask_step(j, carry):
        source = near + j
        for t, step in enumerate(STEPS):
            target = target_row(row, step)
            value = jnp.zeros((BS, LANES), jnp.float32)
            for b in range(4):
                own_range = col * 4 + b
                total = shifts_ref[target, source] + shifts_ref[source, own_range]
                total = (total - shifts_ref[target, own_range]) & (RANGE - 1)
                value = jnp.where(lane_block == b, jnp.where(total == 0, 1.0, 0.0), value)
            masks_ref[t, j] = value.astype(jnp.bfloat16)
        return carry

    lax.fori_loop(0, NEAR, mask_step, 0)


def product_kernel(
    place_ref, shifts_ref, masks, left_0, left_1, left_2, left_3,
    own, before, after, across, twin, twin_others,
    out_0, out_1, out_2, out_3, right, sems,
):
    row = place_ref[0]
    layer = place_ref[2]
    core = row & 1
    zl = (row >> 1) & 3
    near = (row >> 3) * NEAR

    pieces = [(own, 0, core), (before, -1, core), (after, 1, core), (across, 2, core), (twin, 0, 1 - core)]
    pieces += [(twin_others.at[pl.ds(n * RANGE, RANGE)], step, 1 - core) for n, step in enumerate((-1, 1, 2))]
    copies = []
    for n, (piece, step, parity) in enumerate(pieces):
        slot = ((zl + step) & (NZ - 1)) * 2 + parity
        copies.append(pltpu.make_async_copy(piece, right.at[slot], sems.at[n]))
    for copy in copies:
        copy.start()
    for copy in copies:
        copy.wait()

    lefts = [left_0, left_1, left_2, left_3]
    outs = [out_0, out_1, out_2, out_3]

    def position_step(p, carry):
        place = layer * SPAN + p
        for t, step in enumerate(STEPS):
            target = target_row(row, step)
            lhs = jnp.concatenate([lefts[t][0, p], lefts[t][1, p]], axis=1)
            rows = []
            for j in range(NEAR):
                q = (place + shifts_ref[target, near + j]) & (RANGE - 1)
                rows.append(right[j, q] * masks[t, j])
            rhs = jnp.concatenate(rows, axis=0)
            outs[t][p] = jnp.dot(lhs, rhs, preferred_element_type=jnp.float32)
        return carry

    lax.fori_loop(0, SPAN, position_step, 0)


def local(x_blocks, shifts):
    row = lax.axis_index("row")
    col = lax.axis_index("col")
    layer = lax.axis_index("layer")
    x = row // NEAR
    place = jnp.stack([row, col, layer]).astype(jnp.int32)
    smem = pl.BlockSpec(memory_space=pltpu.SMEM)
    vmem = pl.BlockSpec(memory_space=pltpu.VMEM)
    anywhere = pl.BlockSpec(memory_space=pl.ANY)

    before = sent(x_blocks, along_z(1))
    after = sent(x_blocks, along_z(-1))
    across = sent(x_blocks, two_along_z)
    twin = sent(x_blocks, other_core)

    mine = lax.dynamic_slice_in_dim(x_blocks, layer * SPAN, SPAN, 0)
    gathered = lax.all_to_all(jnp.broadcast_to(mine[None], (NY, SPAN, BS, LANES)), "col", 0, 0)

    def columns_of(step):
        return lax.dynamic_slice_in_dim(gathered, ((x + step) % NX) * 2, 2, 0)

    lefts = [columns_of(0)] + [sent(columns_of(step), along_x(step)) for step in STEPS[1:]]
    twin_others = sent(jnp.concatenate([before, after, across], axis=0), other_core)

    masks = pl.pallas_call(
        mask_kernel,
        out_shape=jax.ShapeDtypeStruct((len(STEPS), NEAR, BS, LANES), jnp.bfloat16),
        in_specs=[smem, smem],
        out_specs=vmem,
        name="masks",
    )(place, shifts)
    part = jax.ShapeDtypeStruct((SPAN, BS, LANES), jnp.float32)
    parts = pl.pallas_call(
        product_kernel,
        out_shape=[part] * 4,
        in_specs=[smem, smem] + [vmem] * 5 + [anywhere] * 6,
        out_specs=[vmem] * 4,
        scratch_shapes=[
            pltpu.VMEM((NEAR, RANGE, BS, LANES), jnp.bfloat16),
            pltpu.SemaphoreType.DMA((NEAR,)),
        ],
        compiler_params=pltpu.CompilerParams(vmem_limit_bytes=20 * 1024 * 1024),
        name="range_products",
    )(place, shifts, masks, *lefts, x_blocks, before, after, across, twin, twin_others)
    total = parts[0]
    for part, step in zip(parts[1:], STEPS[1:]):
        total = total + sent(part, along_x(-step))
    return total.astype(jnp.bfloat16)


def solution(mesh):
    return jax.shard_map(
        local,
        mesh=mesh,
        in_specs=(P("row", None, "col"), P()),
        out_specs=P(("row", "layer"), None, "col"),
        check_vma=False,
    )
```

```python
import jax
import jax.numpy as jnp
from jax import lax
from jax.experimental import pallas as pl
from jax.experimental.pallas import tpu as pltpu
from jax.sharding import PartitionSpec as P

AXES = ("row", "col", "layer")
NX, NZ, NY, NL = 4, 4, 8, 4
BS, RANGE, SPAN = 32, 64, 16
LANES = 128
NEAR = 8


def device_pairs(move):
    def index(x, z, core, y):
        return ((x * NZ + z % NZ) * 2 + core) * NY * NL + y * NL + z // NZ

    pairs = []
    for x in range(NX):
        for z in range(NZ * NL):
            for core in range(2):
                for y in range(NY):
                    tx, tz, tcore, ty = move(x, z, core, y)
                    pairs.append((index(x, z, core, y), index(tx % NX, tz % (NZ * NL), tcore, ty % NY)))
    return pairs


def sent(value, move):
    return lax.ppermute(value, AXES, device_pairs(move))


def other_core(x, z, core, y):
    return x, z, 1 - core, y


def along_z(step):
    return lambda x, z, core, y: (x, z + step, core, y)


def two_along_z(x, z, core, y):
    return x, (z + 2 if core == 0 else z - 2), core, y


def swapped_along_x(value):
    groups = [[x * NEAR + n for x in range(NX)] for n in range(NEAR)]
    return lax.all_to_all(value, "row", 0, 0, axis_index_groups=groups)


def mask_kernel(place_ref, shifts_ref, masks_ref):
    row = place_ref[0]
    col = place_ref[1]
    near = (row >> 3) * NEAR
    lane_block = lax.broadcasted_iota(jnp.int32, (BS, LANES), 1) // BS

    def mask_step(j, carry):
        source = near + j
        for t in range(NX):
            target = t * NEAR + (row & (NEAR - 1))
            value = jnp.zeros((BS, LANES), jnp.float32)
            for b in range(4):
                own_range = col * 4 + b
                total = shifts_ref[target, source] + shifts_ref[source, own_range]
                total = (total - shifts_ref[target, own_range]) & (RANGE - 1)
                value = jnp.where(lane_block == b, jnp.where(total == 0, 1.0, 0.0), value)
            masks_ref[t, j] = value.astype(jnp.bfloat16)
        return carry

    lax.fori_loop(0, NEAR, mask_step, 0)


def product_kernel(
    place_ref, shifts_ref, masks, left, own, before, after, across, twin, twin_others, out, right, sems
):
    row = place_ref[0]
    layer = place_ref[2]
    core = row & 1
    zl = (row >> 1) & 3
    near = (row >> 3) * NEAR

    pieces = [(own, 0, core), (before, -1, core), (after, 1, core), (across, 2, core), (twin, 0, 1 - core)]
    pieces += [(twin_others.at[pl.ds(n * RANGE, RANGE)], step, 1 - core) for n, step in enumerate((-1, 1, 2))]
    copies = []
    for n, (piece, step, parity) in enumerate(pieces):
        slot = ((zl + step) & (NZ - 1)) * 2 + parity
        copies.append(pltpu.make_async_copy(piece, right.at[slot], sems.at[n]))
    for copy in copies:
        copy.start()
    for copy in copies:
        copy.wait()

    def position_step(p, carry):
        place = layer * SPAN + p
        for t in range(NX):
            target = t * NEAR + (row & (NEAR - 1))
            lhs = jnp.concatenate([left[t, 0, p], left[t, 1, p]], axis=1)
            rows = []
            for j in range(NEAR):
                q = (place + shifts_ref[target, near + j]) & (RANGE - 1)
                rows.append(right[j, q] * masks[t, j])
            rhs = jnp.concatenate(rows, axis=0)
            out[t, p] = jnp.dot(lhs, rhs, preferred_element_type=jnp.float32)
        return carry

    lax.fori_loop(0, SPAN, position_step, 0)


def local(x_blocks, shifts):
    row = lax.axis_index("row")
    col = lax.axis_index("col")
    layer = lax.axis_index("layer")
    place = jnp.stack([row, col, layer]).astype(jnp.int32)
    smem = pl.BlockSpec(memory_space=pltpu.SMEM)
    vmem = pl.BlockSpec(memory_space=pltpu.VMEM)
    anywhere = pl.BlockSpec(memory_space=pl.ANY)

    mine = lax.dynamic_slice_in_dim(x_blocks, layer * SPAN, SPAN, 0)
    gathered = lax.all_to_all(jnp.broadcast_to(mine[None], (NY, SPAN, BS, LANES)), "col", 0, 0)

    before = sent(x_blocks, along_z(1))
    after = sent(x_blocks, along_z(-1))
    across = sent(x_blocks, two_along_z)
    twin = sent(x_blocks, other_core)
    masks = pl.pallas_call(
        mask_kernel,
        out_shape=jax.ShapeDtypeStruct((NX, NEAR, BS, LANES), jnp.bfloat16),
        in_specs=[smem, smem],
        out_specs=vmem,
        name="masks",
    )(place, shifts)
    before, masks = lax.optimization_barrier((before, masks))
    twin_others = sent(jnp.concatenate([before, after, across], axis=0), other_core)
    left = swapped_along_x(gathered.reshape(NX, 2, SPAN, BS, LANES))

    parts = pl.pallas_call(
        product_kernel,
        out_shape=jax.ShapeDtypeStruct((NX, SPAN, BS, LANES), jnp.float32),
        in_specs=[smem, smem] + [vmem] * 2 + [anywhere] * 6,
        out_specs=vmem,
        scratch_shapes=[
            pltpu.VMEM((NEAR, RANGE, BS, LANES), jnp.bfloat16),
            pltpu.SemaphoreType.DMA((NEAR,)),
        ],
        compiler_params=pltpu.CompilerParams(vmem_limit_bytes=20 * 1024 * 1024),
        name="range_products",
    )(place, shifts, masks, left, x_blocks, before, after, across, twin, twin_others)
    return jnp.sum(swapped_along_x(parts), axis=0).astype(jnp.bfloat16)


def solution(mesh):
    return jax.shard_map(
        local,
        mesh=mesh,
        in_specs=(P("row", None, "col"), P()),
        out_specs=P(("row", "layer"), None, "col"),
        check_vma=False,
    )
```

```python
import jax
import jax.numpy as jnp
from jax import lax
from jax.experimental import pallas as pl
from jax.experimental.pallas import tpu as pltpu
from jax.sharding import PartitionSpec as P

AXES = ("row", "col", "layer")
NX, NZ, NY, NL = 4, 4, 8, 4
BS, RANGE, SPAN = 32, 64, 16
LANES = 128
NEAR = 8


def device_pairs(move):
    def index(x, z, core, y):
        return ((x * NZ + z % NZ) * 2 + core) * NY * NL + y * NL + z // NZ

    pairs = []
    for x in range(NX):
        for z in range(NZ * NL):
            for core in range(2):
                for y in range(NY):
                    tx, tz, tcore, ty = move(x, z, core, y)
                    pairs.append((index(x, z, core, y), index(tx % NX, tz % (NZ * NL), tcore, ty % NY)))
    return pairs


def sent(value, move):
    return lax.ppermute(value, AXES, device_pairs(move))


def other_core(x, z, core, y):
    return x, z, 1 - core, y


def along_z(turn):
    def move(x, z, core, y):
        if core == turn:
            return x, z ^ 1, core, y
        return x, (z + 1 if z % 2 else z - 1), core, y

    return move


def spread(x, z, core, y):
    near_x, side = y // 2, y % 2
    turn = (x - near_x) % NX
    return near_x, z, core, (y + turn if side else y - turn)


def swapped_along_x(value):
    groups = [[x * NEAR + n for x in range(NX)] for n in range(NEAR)]
    return lax.all_to_all(value, "row", 0, 0, axis_index_groups=groups)


def mask_kernel(place_ref, shifts_ref, masks_ref):
    row = place_ref[0]
    col = place_ref[1]
    near = (row >> 3) * NEAR
    lane_block = lax.broadcasted_iota(jnp.int32, (BS, LANES), 1) // BS

    def mask_step(j, carry):
        source = near + j
        for t in range(NX):
            target = t * NEAR + (row & (NEAR - 1))
            value = jnp.zeros((BS, LANES), jnp.float32)
            for b in range(4):
                own_range = col * 4 + b
                total = shifts_ref[target, source] + shifts_ref[source, own_range]
                total = (total - shifts_ref[target, own_range]) & (RANGE - 1)
                value = jnp.where(lane_block == b, jnp.where(total == 0, 1.0, 0.0), value)
            masks_ref[t, j] = value.astype(jnp.bfloat16)
        return carry

    lax.fori_loop(0, NEAR, mask_step, 0)


def product_kernel(
    place_ref, shifts_ref, masks, left, pair, far, twin_pair, twin_far, out, right, sems
):
    row = place_ref[0]
    layer = place_ref[2]
    core = row & 1
    zl = (row >> 1) & 3
    x = row >> 3
    near = x * NEAR

    first = jnp.where(core == 0, 1, 3)
    second = jnp.where(core == 0, 3, 1)
    pieces = [(pair, 0, 0, core), (pair, 1, first, core), (far, 0, second, core), (far, 1, 2, core)]
    pieces += [(twin_pair, 0, 0, 1 - core), (twin_pair, 1, second, 1 - core)]
    pieces += [(twin_far, 0, first, 1 - core), (twin_far, 1, 2, 1 - core)]
    copies = []
    for n, (piece, half, turn, parity) in enumerate(pieces):
        slot = (zl ^ turn) * 2 + parity
        copies.append(pltpu.make_async_copy(piece.at[pl.ds(half * RANGE, RANGE)], right.at[slot], sems.at[n]))
    for copy in copies:
        copy.start()
    for copy in copies:
        copy.wait()

    def position_step(p, carry):
        place = layer * SPAN + p
        for t in range(NX):
            target = t * NEAR + (row & (NEAR - 1))
            turn = (t - x) & (NX - 1)
            low, high = (2 * x - turn) & (NY - 1), (2 * x + 1 + turn) & (NY - 1)
            lhs = jnp.concatenate([left[low, p], left[high, p]], axis=1)
            rows = []
            for j in range(NEAR):
                q = (place + shifts_ref[target, near + j]) & (RANGE - 1)
                rows.append(right[j, q] * masks[t, j])
            rhs = jnp.concatenate(rows, axis=0)
            out[t, p] = jnp.dot(lhs, rhs, preferred_element_type=jnp.float32)
        return carry

    lax.fori_loop(0, SPAN, position_step, 0)


def local(x_blocks, shifts):
    row = lax.axis_index("row")
    col = lax.axis_index("col")
    layer = lax.axis_index("layer")
    place = jnp.stack([row, col, layer]).astype(jnp.int32)
    smem = pl.BlockSpec(memory_space=pltpu.SMEM)
    vmem = pl.BlockSpec(memory_space=pltpu.VMEM)
    anywhere = pl.BlockSpec(memory_space=pl.ANY)

    mine = lax.dynamic_slice_in_dim(x_blocks, layer * SPAN, SPAN, 0)
    mine = sent(mine, spread)
    masks = pl.pallas_call(
        mask_kernel,
        out_shape=jax.ShapeDtypeStruct((NX, NEAR, BS, LANES), jnp.bfloat16),
        in_specs=[smem, smem],
        out_specs=vmem,
        name="masks",
    )(place, shifts)
    near = sent(x_blocks, along_z(0))
    near, masks, mine = lax.optimization_barrier((near, masks, mine))
    left = lax.all_to_all(jnp.broadcast_to(mine[None], (NY, SPAN, BS, LANES)), "col", 0, 0)
    pair = jnp.concatenate([x_blocks, near], axis=0)
    far = sent(pair, along_z(1))
    twin_pair = sent(pair, other_core)
    twin_far = sent(far, other_core)
    parts = pl.pallas_call(
        product_kernel,
        out_shape=jax.ShapeDtypeStruct((NX, SPAN, BS, LANES), jnp.float32),
        in_specs=[smem, smem] + [vmem] * 2 + [anywhere] * 4,
        out_specs=vmem,
        scratch_shapes=[
            pltpu.VMEM((NEAR, RANGE, BS, LANES), jnp.bfloat16),
            pltpu.SemaphoreType.DMA((NEAR,)),
        ],
        compiler_params=pltpu.CompilerParams(vmem_limit_bytes=20 * 1024 * 1024),
        name="range_products",
    )(place, shifts, masks, left, pair, far, twin_pair, twin_far)
    return jnp.sum(swapped_along_x(parts), axis=0).astype(jnp.bfloat16)


def solution(mesh):
    return jax.shard_map(
        local,
        mesh=mesh,
        in_specs=(P("row", None, "col"), P()),
        out_specs=P(("row", "layer"), None, "col"),
        check_vma=False,
    )
```

```python
import jax
import jax.numpy as jnp
from jax import lax
from jax.experimental import pallas as pl
from jax.experimental.pallas import tpu as pltpu
from jax.sharding import PartitionSpec as P

AXES = ("row", "col", "layer")
NX, NZ, NY, NL = 4, 4, 8, 4
BS, RANGE, SPAN = 32, 64, 16
LANES = 128
NEAR = 8


def device_pairs(move):
    def index(x, z, core, y):
        return ((x * NZ + z % NZ) * 2 + core) * NY * NL + y * NL + z // NZ

    pairs = []
    for x in range(NX):
        for z in range(NZ * NL):
            for core in range(2):
                for y in range(NY):
                    tx, tz, tcore, ty = move(x, z, core, y)
                    pairs.append((index(x, z, core, y), index(tx % NX, tz % (NZ * NL), tcore, ty % NY)))
    return pairs


def sent(value, move):
    return lax.ppermute(value, AXES, device_pairs(move))


def other_core(x, z, core, y):
    return x, z, 1 - core, y


def along_z(turn):
    def move(x, z, core, y):
        if core == turn:
            return x, z ^ 1, core, y
        return x, (z + 1 if z % 2 else z - 1), core, y

    return move


def neighbour(y, turn):
    return (y ^ 1 if turn == 0 else ((y + 1) ^ 1) - 1) & (NY - 1)


def along_y(*turns):
    def move(x, z, core, y):
        for turn in turns:
            y = neighbour(y, turn ^ core)
        return x, z, core, y

    return move


def spread(x, z, core, y):
    near_x, side = y // 2, y % 2
    turn = (x - near_x) % NX
    return near_x, z, core, (y + turn if side else y - turn)


def swapped_along_x(value):
    groups = [[x * NEAR + n for x in range(NX)] for n in range(NEAR)]
    return lax.all_to_all(value, "row", 0, 0, axis_index_groups=groups)


def mask_kernel(place_ref, shifts_ref, masks_ref):
    row = place_ref[0]
    col = place_ref[1]
    near = (row >> 3) * NEAR
    lane_block = lax.broadcasted_iota(jnp.int32, (BS, LANES), 1) // BS

    def mask_step(j, carry):
        source = near + j
        for t in range(NX):
            target = t * NEAR + (row & (NEAR - 1))
            value = jnp.zeros((BS, LANES), jnp.float32)
            for b in range(4):
                own_range = col * 4 + b
                total = shifts_ref[target, source] + shifts_ref[source, own_range]
                total = (total - shifts_ref[target, own_range]) & (RANGE - 1)
                value = jnp.where(lane_block == b, jnp.where(total == 0, 1.0, 0.0), value)
            masks_ref[t, j] = value.astype(jnp.bfloat16)
        return carry

    lax.fori_loop(0, NEAR, mask_step, 0)


def product_kernel(
    place_ref, shifts_ref, masks, left_pair, left_far, left_back, left_on, pair, far, twin_pair, twin_far,
    out, left, right, sems,
):
    row = place_ref[0]
    col = place_ref[1]
    layer = place_ref[2]
    core = row & 1
    zl = (row >> 1) & 3
    x = row >> 3
    near = x * NEAR

    first = jnp.where(core == 0, 1, 3)
    second = jnp.where(core == 0, 3, 1)
    pieces = [(pair, 0, 0, core), (pair, 1, first, core), (far, 0, second, core), (far, 1, 2, core)]
    pieces += [(twin_pair, 0, 0, 1 - core), (twin_pair, 1, second, 1 - core)]
    pieces += [(twin_far, 0, first, 1 - core), (twin_far, 1, 2, 1 - core)]
    copies = []
    for n, (piece, half, turn, parity) in enumerate(pieces):
        slot = (zl ^ turn) * 2 + parity
        copies.append(pltpu.make_async_copy(piece.at[pl.ds(half * RANGE, RANGE)], right.at[slot], sems.at[n]))
    def turned(*turns):
        y = col
        for turn in turns:
            y = jnp.where(core == turn, y ^ 1, ((y + 1) ^ 1) - 1) & (NY - 1)
        return y

    lefts = [(left_pair, turned(), turned(0)), (left_far, turned(1), turned(1, 0))]
    lefts += [(left_back, turned(0, 1), turned(0, 1, 0)), (left_on, turned(1, 0, 1), turned(1, 0, 1, 0))]
    for n, (piece, *slots) in enumerate(lefts):
        for half, slot in enumerate(slots):
            from_piece = piece.at[pl.ds(half * SPAN, SPAN)]
            copies.append(pltpu.make_async_copy(from_piece, left.at[slot], sems.at[NEAR + 2 * n + half]))
    for copy in copies:
        copy.start()
    for copy in copies:
        copy.wait()

    def position_step(p, carry):
        place = layer * SPAN + p
        for t in range(NX):
            target = t * NEAR + (row & (NEAR - 1))
            turn = (t - x) & (NX - 1)
            low, high = (2 * x - turn) & (NY - 1), (2 * x + 1 + turn) & (NY - 1)
            lhs = jnp.concatenate([left[low, p], left[high, p]], axis=1)
            rows = []
            for j in range(NEAR):
                q = (place + shifts_ref[target, near + j]) & (RANGE - 1)
                rows.append(right[j, q] * masks[t, j])
            rhs = jnp.concatenate(rows, axis=0)
            out[t, p] = jnp.dot(lhs, rhs, preferred_element_type=jnp.float32)
        return carry

    lax.fori_loop(0, SPAN, position_step, 0)


def local(x_blocks, shifts):
    row = lax.axis_index("row")
    col = lax.axis_index("col")
    layer = lax.axis_index("layer")
    place = jnp.stack([row, col, layer]).astype(jnp.int32)
    smem = pl.BlockSpec(memory_space=pltpu.SMEM)
    vmem = pl.BlockSpec(memory_space=pltpu.VMEM)
    anywhere = pl.BlockSpec(memory_space=pl.ANY)

    mine = lax.dynamic_slice_in_dim(x_blocks, layer * SPAN, SPAN, 0)
    mine = sent(mine, spread)
    masks = pl.pallas_call(
        mask_kernel,
        out_shape=jax.ShapeDtypeStruct((NX, NEAR, BS, LANES), jnp.bfloat16),
        in_specs=[smem, smem],
        out_specs=vmem,
        name="masks",
    )(place, shifts)
    near = sent(x_blocks, along_z(0))
    near, masks, mine = lax.optimization_barrier((near, masks, mine))
    left_next = sent(mine, along_y(0))
    pair = jnp.concatenate([x_blocks, near], axis=0)
    far = sent(pair, along_z(1))
    pair, left_next = lax.optimization_barrier((pair, left_next))
    left_pair = jnp.concatenate([mine, left_next], axis=0)
    left_far = sent(left_pair, along_y(1))
    left_back = sent(left_far, along_y(0))
    left_on = sent(left_far, along_y(0, 1))
    twin_pair = sent(pair, other_core)
    far, left_pair = lax.optimization_barrier((far, left_pair))
    twin_far = sent(far, other_core)
    parts = pl.pallas_call(
        product_kernel,
        out_shape=jax.ShapeDtypeStruct((NX, SPAN, BS, LANES), jnp.float32),
        in_specs=[smem, smem] + [vmem] + [anywhere] * 8,
        out_specs=vmem,
        scratch_shapes=[
            pltpu.VMEM((NY, SPAN, BS, LANES), jnp.bfloat16),
            pltpu.VMEM((NEAR, RANGE, BS, LANES), jnp.bfloat16),
            pltpu.SemaphoreType.DMA((NEAR + NY,)),
        ],
        compiler_params=pltpu.CompilerParams(vmem_limit_bytes=20 * 1024 * 1024),
        name="range_products",
    )(place, shifts, masks, left_pair, left_far, left_back, left_on, pair, far, twin_pair, twin_far)
    return jnp.sum(swapped_along_x(parts), axis=0).astype(jnp.bfloat16)


def solution(mesh):
    return jax.shard_map(
        local,
        mesh=mesh,
        in_specs=(P("row", None, "col"), P()),
        out_specs=P(("row", "layer"), None, "col"),
        check_vma=False,
    )
```

```python
import jax
import jax.numpy as jnp
from jax import lax
from jax.experimental import pallas as pl
from jax.experimental.pallas import tpu as pltpu
from jax.sharding import PartitionSpec as P

AXES = ("row", "col", "layer")
NX, NZ, NY, NL = 4, 4, 8, 4
BS, RANGE, SPAN = 32, 64, 16
LANES = 128
NEAR = 8


def device_pairs(move):
    def index(x, z, core, y):
        return ((x * NZ + z % NZ) * 2 + core) * NY * NL + y * NL + z // NZ

    pairs = []
    for x in range(NX):
        for z in range(NZ * NL):
            for core in range(2):
                for y in range(NY):
                    tx, tz, tcore, ty = move(x, z, core, y)
                    pairs.append((index(x, z, core, y), index(tx % NX, tz % (NZ * NL), tcore, ty % NY)))
    return pairs


def sent(value, move):
    return lax.ppermute(value, AXES, device_pairs(move))


def other_core(x, z, core, y):
    return x, z, 1 - core, y


def along_z(turn):
    def move(x, z, core, y):
        if core == turn:
            return x, z ^ 1, core, y
        return x, (z + 1 if z % 2 else z - 1), core, y

    return move


def neighbour(y, turn):
    return (y ^ 1 if turn == 0 else ((y + 1) ^ 1) - 1) & (NY - 1)


def along_y(*turns):
    def move(x, z, core, y):
        for turn in turns:
            y = neighbour(y, turn ^ core)
        return x, z, core, y

    return move


def spread(x, z, core, y):
    near_x, side = y // 2, y % 2
    turn = (x - near_x) % NX
    return near_x, z, core, (y + turn if side else y - turn)


def swapped_along_x(value):
    groups = [[x * NEAR + n for x in range(NX)] for n in range(NEAR)]
    return lax.all_to_all(value, "row", 0, 0, axis_index_groups=groups)


def mask_kernel(place_ref, shifts_ref, masks_ref):
    row = place_ref[0]
    col = place_ref[1]
    near = (row >> 3) * NEAR
    lane_block = lax.broadcasted_iota(jnp.int32, (BS, LANES), 1) // BS

    def mask_step(j, carry):
        source = near + j
        for t in range(NX):
            target = t * NEAR + (row & (NEAR - 1))
            value = jnp.zeros((BS, LANES), jnp.float32)
            for b in range(4):
                own_range = col * 4 + b
                total = shifts_ref[target, source] + shifts_ref[source, own_range]
                total = (total - shifts_ref[target, own_range]) & (RANGE - 1)
                value = jnp.where(lane_block == b, jnp.where(total == 0, 1.0, 0.0), value)
            masks_ref[t, j] = value.astype(jnp.bfloat16)
        return carry

    lax.fori_loop(0, NEAR, mask_step, 0)


def product_kernel(
    place_ref, shifts_ref, masks, left_pair, left_far, left_back, left_on, near_blocks, twin_blocks,
    out, left, right, sems,
):
    row = place_ref[0]
    col = place_ref[1]
    layer = place_ref[2]
    core = row & 1
    zl = (row >> 1) & 3
    x = row >> 3
    near = x * NEAR

    first = jnp.where(core == 0, 1, 3)
    second = jnp.where(core == 0, 3, 1)
    pieces = [(near_blocks, n, turn, core) for n, turn in enumerate((0, first, second, 2))]
    pieces += [(twin_blocks, n, turn, 1 - core) for n, turn in enumerate((0, second, first, 2))]
    copies = []
    for n, (piece, half, turn, parity) in enumerate(pieces):
        slot = (zl ^ turn) * 2 + parity
        copies.append(pltpu.make_async_copy(piece.at[pl.ds(half * RANGE, RANGE)], right.at[slot], sems.at[n]))
    def turned(*turns):
        y = col
        for turn in turns:
            y = jnp.where(core == turn, y ^ 1, ((y + 1) ^ 1) - 1) & (NY - 1)
        return y

    lefts = [(left_pair, turned(), turned(0)), (left_far, turned(1), turned(1, 0))]
    lefts += [(left_back, turned(0, 1), turned(0, 1, 0)), (left_on, turned(1, 0, 1), turned(1, 0, 1, 0))]
    for n, (piece, *slots) in enumerate(lefts):
        for half, slot in enumerate(slots):
            from_piece = piece.at[pl.ds(half * SPAN, SPAN)]
            copies.append(pltpu.make_async_copy(from_piece, left.at[slot], sems.at[NEAR + 2 * n + half]))
    for copy in copies:
        copy.start()
    for copy in copies:
        copy.wait()

    def position_step(p, carry):
        place = layer * SPAN + p
        for t in range(NX):
            target = t * NEAR + (row & (NEAR - 1))
            turn = (t - x) & (NX - 1)
            low, high = (2 * x - turn) & (NY - 1), (2 * x + 1 + turn) & (NY - 1)
            lhs = jnp.concatenate([left[low, p], left[high, p]], axis=1)
            rows = []
            for j in range(NEAR):
                q = (place + shifts_ref[target, near + j]) & (RANGE - 1)
                rows.append(right[j, q] * masks[t, j])
            rhs = jnp.concatenate(rows, axis=0)
            out[t, p] = jnp.dot(lhs, rhs, preferred_element_type=jnp.float32)
        return carry

    lax.fori_loop(0, SPAN, position_step, 0)


def local(x_blocks, shifts):
    row = lax.axis_index("row")
    col = lax.axis_index("col")
    layer = lax.axis_index("layer")
    place = jnp.stack([row, col, layer]).astype(jnp.int32)
    smem = pl.BlockSpec(memory_space=pltpu.SMEM)
    vmem = pl.BlockSpec(memory_space=pltpu.VMEM)
    anywhere = pl.BlockSpec(memory_space=pl.ANY)

    mine = lax.dynamic_slice_in_dim(x_blocks, layer * SPAN, SPAN, 0)
    mine = sent(mine, spread)
    masks = pl.pallas_call(
        mask_kernel,
        out_shape=jax.ShapeDtypeStruct((NX, NEAR, BS, LANES), jnp.bfloat16),
        in_specs=[smem, smem],
        out_specs=vmem,
        name="masks",
    )(place, shifts)
    near = sent(x_blocks, along_z(0))
    near, masks, mine = lax.optimization_barrier((near, masks, mine))
    left_next = sent(mine, along_y(0))
    pair = jnp.concatenate([x_blocks, near], axis=0)
    far = sent(pair, along_z(1))
    left_pair = jnp.concatenate([mine, left_next], axis=0)
    left_far = sent(left_pair, along_y(1))
    far, left_far = lax.optimization_barrier((far, left_far))
    left_back = sent(left_far, along_y(0))
    left_on = sent(left_far, along_y(0, 1))
    right = jnp.concatenate([pair, far], axis=0)
    twin = sent(right, other_core)
    parts = pl.pallas_call(
        product_kernel,
        out_shape=jax.ShapeDtypeStruct((NX, SPAN, BS, LANES), jnp.float32),
        in_specs=[smem, smem] + [vmem] + [anywhere] * 6,
        out_specs=vmem,
        scratch_shapes=[
            pltpu.VMEM((NY, SPAN, BS, LANES), jnp.bfloat16),
            pltpu.VMEM((NEAR, RANGE, BS, LANES), jnp.bfloat16),
            pltpu.SemaphoreType.DMA((NEAR + NY,)),
        ],
        compiler_params=pltpu.CompilerParams(vmem_limit_bytes=12 * 1024 * 1024),
        name="range_products",
    )(place, shifts, masks, left_pair, left_far, left_back, left_on, right, twin)
    return jnp.sum(swapped_along_x(parts), axis=0).astype(jnp.bfloat16)


def solution(mesh):
    return jax.shard_map(
        local,
        mesh=mesh,
        in_specs=(P("row", None, "col"), P()),
        out_specs=P(("row", "layer"), None, "col"),
        check_vma=False,
    )
```

```python
import jax
import jax.numpy as jnp
from jax import lax
from jax.experimental import pallas as pl
from jax.experimental.pallas import tpu as pltpu
from jax.sharding import PartitionSpec as P

AXES = ("row", "col", "layer")
NX, NZ, NY, NL = 4, 4, 8, 4
BS, RANGE, SPAN = 32, 64, 16
LANES = 128
NEAR = 8


def device_pairs(move):
    def index(x, z, core, y):
        return ((x * NZ + z % NZ) * 2 + core) * NY * NL + y * NL + z // NZ

    pairs = []
    for x in range(NX):
        for z in range(NZ * NL):
            for core in range(2):
                for y in range(NY):
                    target = move(x, z, core, y)
                    if target is None:
                        continue
                    tx, tz, tcore, ty = target
                    pairs.append((index(x, z, core, y), index(tx % NX, tz % (NZ * NL), tcore, ty % NY)))
    return pairs


def sent(value, move):
    return lax.ppermute(value, AXES, device_pairs(move))


def other_core(x, z, core, y):
    return x, z, 1 - core, y


def along_z(turn):
    def move(x, z, core, y):
        target = z ^ 1 if core == turn else (z + 1 if z % 2 else z - 1)
        return (x, target, core, y) if 0 <= target < NZ * NL else None

    return move


def to_ends(turn):
    ends = {NZ - 1: 0, NZ * NL - NZ: NZ * NL - 1}

    def move(x, z, core, y):
        return (x, ends[z], core, y) if core != turn and z in ends else None

    return move


def spread(x, z, core, y):
    near_x, side = y // 2, y % 2
    turn = (x - near_x) % NX
    return near_x, z, core, (y + turn if side else y - turn)


def swapped_along_x(value):
    groups = [[x * NEAR + n for x in range(NX)] for n in range(NEAR)]
    return lax.all_to_all(value, "row", 0, 0, axis_index_groups=groups)


def mask_kernel(place_ref, shifts_ref, masks_ref):
    row = place_ref[0]
    col = place_ref[1]
    near = (row >> 3) * NEAR
    lane_block = lax.broadcasted_iota(jnp.int32, (BS, LANES), 1) // BS

    def mask_step(j, carry):
        source = near + j
        for t in range(NX):
            target = t * NEAR + (row & (NEAR - 1))
            value = jnp.zeros((BS, LANES), jnp.float32)
            for b in range(4):
                own_range = col * 4 + b
                total = shifts_ref[target, source] + shifts_ref[source, own_range]
                total = (total - shifts_ref[target, own_range]) & (RANGE - 1)
                value = jnp.where(lane_block == b, jnp.where(total == 0, 1.0, 0.0), value)
            masks_ref[t, j] = value.astype(jnp.bfloat16)
        return carry

    lax.fori_loop(0, NEAR, mask_step, 0)


def product_kernel(
    place_ref, shifts_ref, masks, left, pair, far, twin_pair, twin_far, out, right, sems
):
    row = place_ref[0]
    layer = place_ref[2]
    core = row & 1
    zl = (row >> 1) & 3
    x = row >> 3
    near = x * NEAR

    first = jnp.where(core == 0, 1, 3)
    second = jnp.where(core == 0, 3, 1)
    pieces = [(pair, 0, 0, core), (pair, 1, first, core), (far, 0, second, core), (far, 1, 2, core)]
    pieces += [(twin_pair, 0, 0, 1 - core), (twin_pair, 1, second, 1 - core)]
    pieces += [(twin_far, 0, first, 1 - core), (twin_far, 1, 2, 1 - core)]
    copies = []
    for n, (piece, half, turn, parity) in enumerate(pieces):
        slot = (zl ^ turn) * 2 + parity
        copies.append(pltpu.make_async_copy(piece.at[pl.ds(half * RANGE, RANGE)], right.at[slot], sems.at[n]))
    for copy in copies:
        copy.start()
    for copy in copies:
        copy.wait()

    def position_step(p, carry):
        place = layer * SPAN + p
        for t in range(NX):
            target = t * NEAR + (row & (NEAR - 1))
            turn = (t - x) & (NX - 1)
            low, high = (2 * x - turn) & (NY - 1), (2 * x + 1 + turn) & (NY - 1)
            lhs = jnp.concatenate([left[low, p], left[high, p]], axis=1)
            rows = []
            for j in range(NEAR):
                q = (place + shifts_ref[target, near + j]) & (RANGE - 1)
                rows.append(right[j, q] * masks[t, j])
            rhs = jnp.concatenate(rows, axis=0)
            out[t, p] = jnp.dot(lhs, rhs, preferred_element_type=jnp.float32)
        return carry

    lax.fori_loop(0, SPAN, position_step, 0)


def local(x_blocks, shifts):
    row = lax.axis_index("row")
    col = lax.axis_index("col")
    layer = lax.axis_index("layer")
    place = jnp.stack([row, col, layer]).astype(jnp.int32)
    smem = pl.BlockSpec(memory_space=pltpu.SMEM)
    vmem = pl.BlockSpec(memory_space=pltpu.VMEM)
    anywhere = pl.BlockSpec(memory_space=pl.ANY)

    mine = lax.dynamic_slice_in_dim(x_blocks, layer * SPAN, SPAN, 0)
    mine = sent(mine, spread)
    masks = pl.pallas_call(
        mask_kernel,
        out_shape=jax.ShapeDtypeStruct((NX, NEAR, BS, LANES), jnp.bfloat16),
        in_specs=[smem, smem],
        out_specs=vmem,
        name="masks",
    )(place, shifts)
    near = sent(x_blocks, along_z(0)) + sent(x_blocks, to_ends(0))
    near, masks, mine = lax.optimization_barrier((near, masks, mine))
    left = lax.all_to_all(jnp.broadcast_to(mine[None], (NY, SPAN, BS, LANES)), "col", 0, 0)
    pair = jnp.concatenate([x_blocks, near], axis=0)
    far = sent(pair, along_z(1)) + sent(pair, to_ends(1))
    twin_pair = sent(pair, other_core)
    twin_far = sent(far, other_core)
    parts = pl.pallas_call(
        product_kernel,
        out_shape=jax.ShapeDtypeStruct((NX, SPAN, BS, LANES), jnp.float32),
        in_specs=[smem, smem] + [vmem] * 2 + [anywhere] * 4,
        out_specs=vmem,
        scratch_shapes=[
            pltpu.VMEM((NEAR, RANGE, BS, LANES), jnp.bfloat16),
            pltpu.SemaphoreType.DMA((NEAR,)),
        ],
        compiler_params=pltpu.CompilerParams(vmem_limit_bytes=12 * 1024 * 1024),
        name="range_products",
    )(place, shifts, masks, left, pair, far, twin_pair, twin_far)
    return jnp.sum(swapped_along_x(parts), axis=0).astype(jnp.bfloat16)


def solution(mesh):
    return jax.shard_map(
        local,
        mesh=mesh,
        in_specs=(P("row", None, "col"), P()),
        out_specs=P(("row", "layer"), None, "col"),
        check_vma=False,
    )
```

```python
import jax
import jax.numpy as jnp
from jax import lax
from jax.experimental import pallas as pl
from jax.experimental.pallas import tpu as pltpu
from jax.sharding import PartitionSpec as P

AXES = ("row", "col", "layer")
NX, NZ, NY, NL = 4, 4, 8, 4
BS, RANGE, SPAN = 32, 64, 16
LANES = 128
NEAR = 8


def device_pairs(move):
    def index(x, z, core, y):
        return ((x * NZ + z % NZ) * 2 + core) * NY * NL + y * NL + z // NZ

    pairs = []
    for x in range(NX):
        for z in range(NZ * NL):
            for core in range(2):
                for y in range(NY):
                    target = move(x, z, core, y)
                    if target is None:
                        continue
                    tx, tz, tcore, ty = target
                    pairs.append((index(x, z, core, y), index(tx % NX, tz % (NZ * NL), tcore, ty % NY)))
    return pairs


def sent(value, move):
    return lax.ppermute(value, AXES, device_pairs(move))


def other_core(x, z, core, y):
    return x, z, 1 - core, y


def along_z(turn):
    def move(x, z, core, y):
        target = z ^ 1 if core == turn else (z + 1 if z % 2 else z - 1)
        return (x, target, core, y) if 0 <= target < NZ * NL else None

    return move


def to_ends(turn):
    ends = {NZ - 1: 0, NZ * NL - NZ: NZ * NL - 1}

    def move(x, z, core, y):
        return (x, ends[z], core, y) if core != turn and z in ends else None

    return move


def spread(x, z, core, y):
    near_x, side = y // 2, y % 2
    turn = (x - near_x) % NX
    return near_x, z, core, (y + turn if side else y - turn)


def along_x(turn):
    return lambda x, z, core, y: (x ^ (1 if core == turn else 3), z, core, y)


def mask_kernel(place_ref, shifts_ref, masks_ref):
    row = place_ref[0]
    col = place_ref[1]
    near = (row >> 3) * NEAR
    lane_block = lax.broadcasted_iota(jnp.int32, (BS, LANES), 1) // BS

    def mask_step(j, carry):
        source = near + j
        for t in range(NX):
            target = t * NEAR + (row & (NEAR - 1))
            value = jnp.zeros((BS, LANES), jnp.float32)
            for b in range(4):
                own_range = col * 4 + b
                total = shifts_ref[target, source] + shifts_ref[source, own_range]
                total = (total - shifts_ref[target, own_range]) & (RANGE - 1)
                value = jnp.where(lane_block == b, jnp.where(total == 0, 1.0, 0.0), value)
            masks_ref[t, j] = value.astype(jnp.bfloat16)
        return carry

    lax.fori_loop(0, NEAR, mask_step, 0)


def add_targets(place_ref, shifts_ref, masks, left, right, out, turns):
    row = place_ref[0]
    layer = place_ref[2]
    x = row >> 3

    def position_step(p, carry):
        place = layer * SPAN + p
        for n, turn in enumerate(turns):
            target = x ^ turn
            target_row = target * NEAR + (row & (NEAR - 1))
            steps = (target - x) & (NX - 1)
            low, high = (2 * x - steps) & (NY - 1), (2 * x + 1 + steps) & (NY - 1)
            lhs = jnp.concatenate([left[low, p], left[high, p]], axis=1)
            rows = []
            for j in range(NEAR):
                q = (place + shifts_ref[target_row, x * NEAR + j]) & (RANGE - 1)
                rows.append(right[j, q] * masks[target, j])
            rhs = jnp.concatenate(rows, axis=0)
            out[n, p] = jnp.dot(lhs, rhs, preferred_element_type=jnp.float32)
        return carry

    lax.fori_loop(0, SPAN, position_step, 0)


def turns_of(place_ref):
    core = place_ref[0] & 1
    return jnp.where(core == 0, 1, 3), jnp.where(core == 0, 3, 1)


def sent_kernel(place_ref, shifts_ref, masks, left, pair, far, twin_pair, twin_far, right, out, sems):
    core = place_ref[0] & 1
    zl = (place_ref[0] >> 1) & 3
    first, second = turns_of(place_ref)
    pieces = [(pair, 0, 0, core), (pair, 1, first, core), (far, 0, second, core), (far, 1, 2, core)]
    pieces += [(twin_pair, 0, 0, 1 - core), (twin_pair, 1, second, 1 - core)]
    pieces += [(twin_far, 0, first, 1 - core), (twin_far, 1, 2, 1 - core)]
    copies = []
    for n, (piece, half, turn, parity) in enumerate(pieces):
        slot = (zl ^ turn) * 2 + parity
        copies.append(pltpu.make_async_copy(piece.at[pl.ds(half * RANGE, RANGE)], right.at[slot], sems.at[n]))
    for copy in copies:
        copy.start()
    for copy in copies:
        copy.wait()
    add_targets(place_ref, shifts_ref, masks, left, right, out, (first, 2))


def kept_kernel(place_ref, shifts_ref, masks, left, right, out):
    add_targets(place_ref, shifts_ref, masks, left, right, out, (0, turns_of(place_ref)[1]))


def local(x_blocks, shifts):
    row = lax.axis_index("row")
    col = lax.axis_index("col")
    layer = lax.axis_index("layer")
    place = jnp.stack([row, col, layer]).astype(jnp.int32)
    smem = pl.BlockSpec(memory_space=pltpu.SMEM)
    vmem = pl.BlockSpec(memory_space=pltpu.VMEM)
    anywhere = pl.BlockSpec(memory_space=pl.ANY)

    mine = lax.dynamic_slice_in_dim(x_blocks, layer * SPAN, SPAN, 0)
    mine = sent(mine, spread)
    masks = pl.pallas_call(
        mask_kernel,
        out_shape=jax.ShapeDtypeStruct((NX, NEAR, BS, LANES), jnp.bfloat16),
        in_specs=[smem, smem],
        out_specs=vmem,
        name="masks",
    )(place, shifts)
    near = sent(x_blocks, along_z(0)) + sent(x_blocks, to_ends(0))
    near, masks, mine = lax.optimization_barrier((near, masks, mine))
    left = lax.all_to_all(jnp.broadcast_to(mine[None], (NY, SPAN, BS, LANES)), "col", 0, 0)
    pair = jnp.concatenate([x_blocks, near], axis=0)
    far = sent(pair, along_z(1)) + sent(pair, to_ends(1))
    twin_pair = sent(pair, other_core)
    twin_far = sent(far, other_core)
    part = jax.ShapeDtypeStruct((2, SPAN, BS, LANES), jnp.float32)
    cost = pl.CostEstimate(flops=NX * 2 ** 25, bytes_accessed=6 * 2 ** 20, transcendentals=0)
    params = pltpu.CompilerParams(vmem_limit_bytes=12 * 1024 * 1024)
    gathered, leaving = pl.pallas_call(
        sent_kernel,
        out_shape=[jax.ShapeDtypeStruct((NEAR, RANGE, BS, LANES), jnp.bfloat16), part],
        in_specs=[smem, smem] + [vmem] * 2 + [anywhere] * 4,
        out_specs=[vmem] * 2,
        scratch_shapes=[pltpu.SemaphoreType.DMA((NEAR,))],
        compiler_params=params,
        cost_estimate=cost,
        name="sent_products",
    )(place, shifts, masks, left, pair, far, twin_pair, twin_far)
    arrived = sent(leaving, along_x(0))
    kept = pl.pallas_call(
        kept_kernel,
        out_shape=part,
        in_specs=[smem, smem] + [vmem] * 3,
        out_specs=vmem,
        compiler_params=params,
        cost_estimate=cost,
        name="kept_products",
    )(place, shifts, masks, left, gathered)
    last = sent(kept[1] + arrived[1], along_x(1))
    return (kept[0] + arrived[0] + last).astype(jnp.bfloat16)


def solution(mesh):
    return jax.shard_map(
        local,
        mesh=mesh,
        in_specs=(P("row", None, "col"), P()),
        out_specs=P(("row", "layer"), None, "col"),
        check_vma=False,
    )
```

```python
import jax
import jax.numpy as jnp
from jax import lax
from jax.experimental import pallas as pl
from jax.experimental.pallas import tpu as pltpu
from jax.sharding import PartitionSpec as P

AXES = ("row", "col", "layer")
NX, NZ, NY, NL = 4, 4, 8, 4
BS, RANGE, SPAN = 32, 64, 16
LANES = 128
NEAR = 8


def device_pairs(move):
    def index(x, z, core, y):
        return ((x * NZ + z % NZ) * 2 + core) * NY * NL + y * NL + z // NZ

    pairs = []
    for x in range(NX):
        for z in range(NZ * NL):
            for core in range(2):
                for y in range(NY):
                    tx, tz, tcore, ty = move(x, z, core, y)
                    pairs.append((index(x, z, core, y), index(tx % NX, tz % (NZ * NL), tcore, ty % NY)))
    return pairs


def sent(value, move):
    return lax.ppermute(value, AXES, device_pairs(move))


def other_core(x, z, core, y):
    return x, z, 1 - core, y


def along_z(turn):
    return lambda x, z, core, y: (x, z ^ (1 if core == turn else 3), core, y)


def spread(x, z, core, y):
    near_x, side = y // 2, y % 2
    turn = (x - near_x) % NX
    return near_x, z, core, (y + turn if side else y - turn)


def swapped_along_x(value):
    groups = [[x * NEAR + n for x in range(NX)] for n in range(NEAR)]
    return lax.all_to_all(value, "row", 0, 0, axis_index_groups=groups)


def mask_kernel(place_ref, shifts_ref, masks_ref):
    row = place_ref[0]
    col = place_ref[1]
    near = (row >> 3) * NEAR
    lane_block = lax.broadcasted_iota(jnp.int32, (BS, LANES), 1) // BS

    def mask_step(j, carry):
        source = near + j
        for t in range(NX):
            target = t * NEAR + (row & (NEAR - 1))
            value = jnp.zeros((BS, LANES), jnp.float32)
            for b in range(4):
                own_range = col * 4 + b
                total = shifts_ref[target, source] + shifts_ref[source, own_range]
                total = (total - shifts_ref[target, own_range]) & (RANGE - 1)
                value = jnp.where(lane_block == b, jnp.where(total == 0, 1.0, 0.0), value)
            masks_ref[t, j] = value.astype(jnp.bfloat16)
        return carry

    lax.fori_loop(0, NEAR, mask_step, 0)


def product_kernel(
    place_ref, shifts_ref, masks, left, pair, far, twin_pair, twin_far, out, right, sems
):
    row = place_ref[0]
    layer = place_ref[2]
    core = row & 1
    zl = (row >> 1) & 3
    x = row >> 3
    near = x * NEAR

    first = jnp.where(core == 0, 1, 3)
    second = jnp.where(core == 0, 3, 1)
    pieces = [(pair, 0, 0, core), (pair, 1, first, core), (far, 0, second, core), (far, 1, 2, core)]
    pieces += [(twin_pair, 0, 0, 1 - core), (twin_pair, 1, second, 1 - core)]
    pieces += [(twin_far, 0, first, 1 - core), (twin_far, 1, 2, 1 - core)]
    copies = []
    for n, (piece, half, turn, parity) in enumerate(pieces):
        slot = (zl ^ turn) * 2 + parity
        copies.append(pltpu.make_async_copy(piece.at[pl.ds(half * RANGE, RANGE)], right.at[slot], sems.at[n]))
    for copy in copies:
        copy.start()
    for copy in copies:
        copy.wait()

    def position_step(p, carry):
        place = layer * SPAN + p
        for t in range(NX):
            target = t * NEAR + (row & (NEAR - 1))
            turn = (t - x) & (NX - 1)
            low, high = (2 * x - turn) & (NY - 1), (2 * x + 1 + turn) & (NY - 1)
            lhs = jnp.concatenate([left[low, p], left[high, p]], axis=1)
            rows = []
            for j in range(NEAR):
                q = (place + shifts_ref[target, near + j]) & (RANGE - 1)
                rows.append(right[j, q] * masks[t, j])
            rhs = jnp.concatenate(rows, axis=0)
            out[t, p] = jnp.dot(lhs, rhs, preferred_element_type=jnp.float32)
        return carry

    lax.fori_loop(0, SPAN, position_step, 0)


def local(x_blocks, shifts):
    row = lax.axis_index("row")
    col = lax.axis_index("col")
    layer = lax.axis_index("layer")
    place = jnp.stack([row, col, layer]).astype(jnp.int32)
    smem = pl.BlockSpec(memory_space=pltpu.SMEM)
    vmem = pl.BlockSpec(memory_space=pltpu.VMEM)
    anywhere = pl.BlockSpec(memory_space=pl.ANY)

    mine = lax.dynamic_slice_in_dim(x_blocks, layer * SPAN, SPAN, 0)
    mine = sent(mine, spread)
    masks = pl.pallas_call(
        mask_kernel,
        out_shape=jax.ShapeDtypeStruct((NX, NEAR, BS, LANES), jnp.bfloat16),
        in_specs=[smem, smem],
        out_specs=vmem,
        name="masks",
    )(place, shifts)
    near = sent(x_blocks, along_z(0))
    near, masks, mine = lax.optimization_barrier((near, masks, mine))
    left = lax.all_to_all(jnp.broadcast_to(mine[None], (NY, SPAN, BS, LANES)), "col", 0, 0)
    pair = jnp.concatenate([x_blocks, near], axis=0)
    far = sent(pair, along_z(1))
    twin_pair = sent(pair, other_core)
    twin_far = sent(far, other_core)
    parts = pl.pallas_call(
        product_kernel,
        out_shape=jax.ShapeDtypeStruct((NX, SPAN, BS, LANES), jnp.float32),
        in_specs=[smem, smem] + [vmem] * 2 + [anywhere] * 4,
        out_specs=vmem,
        scratch_shapes=[
            pltpu.VMEM((NEAR, RANGE, BS, LANES), jnp.bfloat16),
            pltpu.SemaphoreType.DMA((NEAR,)),
        ],
        compiler_params=pltpu.CompilerParams(vmem_limit_bytes=12 * 1024 * 1024),
        name="range_products",
    )(place, shifts, masks, left, pair, far, twin_pair, twin_far)
    return jnp.sum(swapped_along_x(parts), axis=0).astype(jnp.bfloat16)


def solution(mesh):
    return jax.shard_map(
        local,
        mesh=mesh,
        in_specs=(P("row", None, "col"), P()),
        out_specs=P(("row", "layer"), None, "col"),
        check_vma=False,
    )
```

```python
import jax
import jax.numpy as jnp
from jax import lax
from jax.experimental import pallas as pl
from jax.experimental.pallas import tpu as pltpu
from jax.sharding import PartitionSpec as P

AXES = ("row", "col", "layer")
NX, NZ, NY, NL = 4, 4, 8, 4
BS, RANGE, SPAN = 32, 64, 16
LANES = 128
NEAR = 8


def device_pairs(move):
    def index(x, z, core, y):
        return ((x * NZ + z % NZ) * 2 + core) * NY * NL + y * NL + z // NZ

    pairs = []
    for x in range(NX):
        for z in range(NZ * NL):
            for core in range(2):
                for y in range(NY):
                    tx, tz, tcore, ty = move(x, z, core, y)
                    pairs.append((index(x, z, core, y), index(tx % NX, tz % (NZ * NL), tcore, ty % NY)))
    return pairs


def sent(value, move):
    return lax.ppermute(value, AXES, device_pairs(move))


def other_core(x, z, core, y):
    return x, z, 1 - core, y


def along_z(turn):
    return lambda x, z, core, y: (x, z ^ (1 if core == turn else 3), core, y)


def spread(x, z, core, y):
    near_x, side = y // 2, y % 2
    turn = (x - near_x) % NX
    return near_x, z, core, (y + turn if side else y - turn)


def swapped_along_x(value):
    groups = [[x * NEAR + n for x in range(NX)] for n in range(NEAR)]
    return lax.all_to_all(value, "row", 0, 0, axis_index_groups=groups)


def mask_kernel(place_ref, shifts_ref, masks_ref):
    row = place_ref[0]
    col = place_ref[1]
    near = (row >> 3) * NEAR
    lane_block = lax.broadcasted_iota(jnp.int32, (BS, LANES), 1) // BS

    def mask_step(j, carry):
        source = near + j
        for t in range(NX):
            target = t * NEAR + (row & (NEAR - 1))
            value = jnp.zeros((BS, LANES), jnp.float32)
            for b in range(4):
                own_range = col * 4 + b
                total = shifts_ref[target, source] + shifts_ref[source, own_range]
                total = (total - shifts_ref[target, own_range]) & (RANGE - 1)
                value = jnp.where(lane_block == b, jnp.where(total == 0, 1.0, 0.0), value)
            masks_ref[t, j] = value.astype(jnp.bfloat16)
        return carry

    lax.fori_loop(0, NEAR, mask_step, 0)


def product_kernel(
    place_ref, shifts_ref, masks, left, own, near, far, last, twins, twin_last, out, right, sems
):
    row = place_ref[0]
    layer = place_ref[2]
    core = row & 1
    zl = (row >> 1) & 3
    x = row >> 3
    base = x * NEAR

    first = jnp.where(core == 0, 1, 3)
    second = jnp.where(core == 0, 3, 1)
    pieces = [(own, 0, 0, core), (near, 0, first, core), (far, 0, second, core), (last, 0, 2, core)]
    pieces += [(twins, n, turn, 1 - core) for n, turn in enumerate((0, second, first))]
    pieces += [(twin_last, 0, 2, 1 - core)]
    copies = []
    for n, (piece, block, turn, parity) in enumerate(pieces):
        slot = (zl ^ turn) * 2 + parity
        copies.append(pltpu.make_async_copy(piece.at[pl.ds(block * RANGE, RANGE)], right.at[slot], sems.at[n]))
    for copy in copies:
        copy.start()
    for copy in copies:
        copy.wait()

    def position_step(p, carry):
        place = layer * SPAN + p
        for t in range(NX):
            target = t * NEAR + (row & (NEAR - 1))
            turn = (t - x) & (NX - 1)
            low, high = (2 * x - turn) & (NY - 1), (2 * x + 1 + turn) & (NY - 1)
            lhs = jnp.concatenate([left[low, p], left[high, p]], axis=1)
            rows = []
            for j in range(NEAR):
                q = (place + shifts_ref[target, base + j]) & (RANGE - 1)
                rows.append(right[j, q] * masks[t, j])
            rhs = jnp.concatenate(rows, axis=0)
            out[t, p] = jnp.dot(lhs, rhs, preferred_element_type=jnp.float32)
        return carry

    lax.fori_loop(0, SPAN, position_step, 0)


def local(x_blocks, shifts):
    row = lax.axis_index("row")
    col = lax.axis_index("col")
    layer = lax.axis_index("layer")
    place = jnp.stack([row, col, layer]).astype(jnp.int32)
    smem = pl.BlockSpec(memory_space=pltpu.SMEM)
    vmem = pl.BlockSpec(memory_space=pltpu.VMEM)
    anywhere = pl.BlockSpec(memory_space=pl.ANY)

    mine = lax.dynamic_slice_in_dim(x_blocks, layer * SPAN, SPAN, 0)
    mine = sent(mine, spread)
    masks = pl.pallas_call(
        mask_kernel,
        out_shape=jax.ShapeDtypeStruct((NX, NEAR, BS, LANES), jnp.bfloat16),
        in_specs=[smem, smem],
        out_specs=vmem,
        name="masks",
    )(place, shifts)
    near = sent(x_blocks, along_z(0))
    far = sent(x_blocks, along_z(1))
    mine = jnp.broadcast_to(mine[None], (NY, SPAN, BS, LANES))
    near, masks = lax.optimization_barrier((near, masks))
    left = lax.all_to_all(mine, "col", 0, 0)
    last = sent(near, along_z(1))
    twins = sent(jnp.concatenate([x_blocks, near, far], axis=0), other_core)
    twin_last = sent(last, other_core)
    parts = pl.pallas_call(
        product_kernel,
        out_shape=jax.ShapeDtypeStruct((NX, SPAN, BS, LANES), jnp.float32),
        in_specs=[smem, smem] + [vmem] * 2 + [anywhere] * 6,
        out_specs=vmem,
        scratch_shapes=[
            pltpu.VMEM((NEAR, RANGE, BS, LANES), jnp.bfloat16),
            pltpu.SemaphoreType.DMA((NEAR,)),
        ],
        compiler_params=pltpu.CompilerParams(vmem_limit_bytes=12 * 1024 * 1024),
        name="range_products",
    )(place, shifts, masks, left, x_blocks, near, far, last, twins, twin_last)
    return jnp.sum(swapped_along_x(parts), axis=0).astype(jnp.bfloat16)


def solution(mesh):
    return jax.shard_map(
        local,
        mesh=mesh,
        in_specs=(P("row", None, "col"), P()),
        out_specs=P(("row", "layer"), None, "col"),
        check_vma=False,
    )
```

```python
import jax
import jax.numpy as jnp
from jax import lax
from jax.experimental import pallas as pl
from jax.experimental.pallas import tpu as pltpu
from jax.sharding import PartitionSpec as P

AXES = ("row", "col", "layer")
NX, NZ, NY, NL = 4, 4, 8, 4
BS, RANGE, SPAN = 32, 64, 16
LANES = 128
NEAR = 8


def device_pairs(move):
    def index(x, z, core, y):
        return ((x * NZ + z % NZ) * 2 + core) * NY * NL + y * NL + z // NZ

    pairs = []
    for x in range(NX):
        for z in range(NZ * NL):
            for core in range(2):
                for y in range(NY):
                    tx, tz, tcore, ty = move(x, z, core, y)
                    pairs.append((index(x, z, core, y), index(tx % NX, tz % (NZ * NL), tcore, ty % NY)))
    return pairs


def sent(value, move):
    return lax.ppermute(value, AXES, device_pairs(move))


def other_core(x, z, core, y):
    return x, z, 1 - core, y


def along_z(turn):
    return lambda x, z, core, y: (x, z ^ (1 if core == turn else 3), core, y)


def spread(x, z, core, y):
    near_x, side = y // 2, y % 2
    turn = (x - near_x) % NX
    return near_x, z, core, (y + turn if side else y - turn)


def swapped_along_x(value):
    groups = [[x * NEAR + n for x in range(NX)] for n in range(NEAR)]
    return lax.all_to_all(value, "row", 0, 0, axis_index_groups=groups)


def mask_kernel(place_ref, shifts_ref, masks_ref):
    row = place_ref[0]
    col = place_ref[1]
    near = (row >> 3) * NEAR
    lane_block = lax.broadcasted_iota(jnp.int32, (BS, LANES), 1) // BS

    def mask_step(j, carry):
        source = near + j
        for t in range(NX):
            target = t * NEAR + (row & (NEAR - 1))
            value = jnp.zeros((BS, LANES), jnp.float32)
            for b in range(4):
                own_range = col * 4 + b
                total = shifts_ref[target, source] + shifts_ref[source, own_range]
                total = (total - shifts_ref[target, own_range]) & (RANGE - 1)
                value = jnp.where(lane_block == b, jnp.where(total == 0, 1.0, 0.0), value)
            masks_ref[t, j] = value.astype(jnp.bfloat16)
        return carry

    lax.fori_loop(0, NEAR, mask_step, 0)


def product_kernel(
    place_ref, shifts_ref, masks, left, own, near, far, last, twins, twin_last, out, right, sems
):
    row = place_ref[0]
    layer = place_ref[2]
    core = row & 1
    zl = (row >> 1) & 3
    x = row >> 3
    base = x * NEAR

    first = jnp.where(core == 0, 1, 3)
    second = jnp.where(core == 0, 3, 1)
    pieces = [(own, 0, 0, core), (near, 0, first, core), (far, 0, second, core), (last, 0, 2, core)]
    pieces += [(twins, 0, 0, 1 - core), (twins, 1, second, 1 - core)]
    pieces += [(twin_last, 0, first, 1 - core), (twin_last, 1, 2, 1 - core)]
    copies = []
    for n, (piece, block, turn, parity) in enumerate(pieces):
        slot = (zl ^ turn) * 2 + parity
        copies.append(pltpu.make_async_copy(piece.at[pl.ds(block * RANGE, RANGE)], right.at[slot], sems.at[n]))
    for copy in copies:
        copy.start()
    for copy in copies:
        copy.wait()

    def position_step(p, carry):
        place = layer * SPAN + p
        for t in range(NX):
            target = t * NEAR + (row & (NEAR - 1))
            turn = (t - x) & (NX - 1)
            low, high = (2 * x - turn) & (NY - 1), (2 * x + 1 + turn) & (NY - 1)
            lhs = jnp.concatenate([left[low, p], left[high, p]], axis=1)
            rows = []
            for j in range(NEAR):
                q = (place + shifts_ref[target, base + j]) & (RANGE - 1)
                rows.append(right[j, q] * masks[t, j])
            rhs = jnp.concatenate(rows, axis=0)
            out[t, p] = jnp.dot(lhs, rhs, preferred_element_type=jnp.float32)
        return carry

    lax.fori_loop(0, SPAN, position_step, 0)


def local(x_blocks, shifts):
    row = lax.axis_index("row")
    col = lax.axis_index("col")
    layer = lax.axis_index("layer")
    place = jnp.stack([row, col, layer]).astype(jnp.int32)
    smem = pl.BlockSpec(memory_space=pltpu.SMEM)
    vmem = pl.BlockSpec(memory_space=pltpu.VMEM)
    anywhere = pl.BlockSpec(memory_space=pl.ANY)

    mine = lax.dynamic_slice_in_dim(x_blocks, layer * SPAN, SPAN, 0)
    mine = sent(mine, spread)
    masks = pl.pallas_call(
        mask_kernel,
        out_shape=jax.ShapeDtypeStruct((NX, NEAR, BS, LANES), jnp.bfloat16),
        in_specs=[smem, smem],
        out_specs=vmem,
        name="masks",
    )(place, shifts)
    near = sent(x_blocks, along_z(0))
    far = sent(x_blocks, along_z(1))
    mine = jnp.broadcast_to(mine[None], (NY, SPAN, BS, LANES))
    near, far, masks = lax.optimization_barrier((near, far, masks))
    left = lax.all_to_all(mine, "col", 0, 0)
    last = sent(near, along_z(1))
    twins = sent(jnp.concatenate([x_blocks, near], axis=0), other_core)
    twin_last = sent(jnp.concatenate([far, last], axis=0), other_core)
    parts = pl.pallas_call(
        product_kernel,
        out_shape=jax.ShapeDtypeStruct((NX, SPAN, BS, LANES), jnp.float32),
        in_specs=[smem, smem] + [vmem] * 2 + [anywhere] * 6,
        out_specs=vmem,
        scratch_shapes=[
            pltpu.VMEM((NEAR, RANGE, BS, LANES), jnp.bfloat16),
            pltpu.SemaphoreType.DMA((NEAR,)),
        ],
        compiler_params=pltpu.CompilerParams(vmem_limit_bytes=12 * 1024 * 1024),
        name="range_products",
    )(place, shifts, masks, left, x_blocks, near, far, last, twins, twin_last)
    return jnp.sum(swapped_along_x(parts), axis=0).astype(jnp.bfloat16)


def solution(mesh):
    return jax.shard_map(
        local,
        mesh=mesh,
        in_specs=(P("row", None, "col"), P()),
        out_specs=P(("row", "layer"), None, "col"),
        check_vma=False,
    )
```

```python
import jax
import jax.numpy as jnp
from jax import lax
from jax.experimental import pallas as pl
from jax.experimental.pallas import tpu as pltpu
from jax.sharding import PartitionSpec as P

AXES = ("row", "col", "layer")
NX, NZ, NY, NL = 4, 4, 8, 4
BS, RANGE, SPAN = 32, 64, 16
LANES = 128
NEAR = 8


def device_pairs(move):
    def index(x, z, core, y):
        return ((x * NZ + z % NZ) * 2 + core) * NY * NL + y * NL + z // NZ

    pairs = []
    for x in range(NX):
        for z in range(NZ * NL):
            for core in range(2):
                for y in range(NY):
                    tx, tz, tcore, ty = move(x, z, core, y)
                    pairs.append((index(x, z, core, y), index(tx % NX, tz % (NZ * NL), tcore, ty % NY)))
    return pairs


def sent(value, move):
    return lax.ppermute(value, AXES, device_pairs(move))


def other_core(x, z, core, y):
    return x, z, 1 - core, y


def along_z(turn):
    return lambda x, z, core, y: (x, z ^ (1 if core == turn else 3), core, y)


def spread(x, z, core, y):
    near_x, side = y // 2, y % 2
    turn = (x - near_x) % NX
    return near_x, z, core, (y + turn if side else y - turn)


def swapped_along_x(value):
    groups = [[x * NEAR + n for x in range(NX)] for n in range(NEAR)]
    return lax.all_to_all(value, "row", 0, 0, axis_index_groups=groups)


def mask_kernel(place_ref, shifts_ref, masks_ref):
    row = place_ref[0]
    col = place_ref[1]
    near = (row >> 3) * NEAR
    lane_block = lax.broadcasted_iota(jnp.int32, (BS, LANES), 1) // BS

    def mask_step(j, carry):
        source = near + j
        for t in range(NX):
            target = t * NEAR + (row & (NEAR - 1))
            value = jnp.zeros((BS, LANES), jnp.float32)
            for b in range(4):
                own_range = col * 4 + b
                total = shifts_ref[target, source] + shifts_ref[source, own_range]
                total = (total - shifts_ref[target, own_range]) & (RANGE - 1)
                value = jnp.where(lane_block == b, jnp.where(total == 0, 1.0, 0.0), value)
            masks_ref[t, j] = value.astype(jnp.bfloat16)
        return carry

    lax.fori_loop(0, NEAR, mask_step, 0)


def product_kernel(
    place_ref, shifts_ref, masks, left, own, near, far, last, twins, twin_last, out, right, sems
):
    row = place_ref[0]
    layer = place_ref[2]
    core = row & 1
    zl = (row >> 1) & 3
    x = row >> 3
    base = x * NEAR

    first = jnp.where(core == 0, 1, 3)
    second = jnp.where(core == 0, 3, 1)
    pieces = [(own, 0, 0, core), (near, 0, first, core), (far, 0, second, core), (last, 0, 2, core)]
    pieces += [(twins, 0, 0, 1 - core), (twins, 1, second, 1 - core)]
    pieces += [(twin_last, 0, first, 1 - core), (twin_last, 1, 2, 1 - core)]
    copies = []
    for n, (piece, block, turn, parity) in enumerate(pieces):
        slot = (zl ^ turn) * 2 + parity
        copies.append(pltpu.make_async_copy(piece.at[pl.ds(block * RANGE, RANGE)], right.at[slot], sems.at[n]))
    for copy in copies:
        copy.start()
    for copy in copies:
        copy.wait()

    def position_step(p, carry):
        place = layer * SPAN + p
        for t in range(NX):
            target = t * NEAR + (row & (NEAR - 1))
            turn = (t - x) & (NX - 1)
            low, high = (2 * x - turn) & (NY - 1), (2 * x + 1 + turn) & (NY - 1)
            lhs = jnp.concatenate([left[low, p], left[high, p]], axis=1)
            rows = []
            for j in range(NEAR):
                q = (place + shifts_ref[target, base + j]) & (RANGE - 1)
                rows.append(right[j, q] * masks[t, j])
            rhs = jnp.concatenate(rows, axis=0)
            out[t, p] = jnp.dot(lhs, rhs, preferred_element_type=jnp.float32)
        return carry

    lax.fori_loop(0, SPAN, position_step, 0)


def local(x_blocks, shifts):
    row = lax.axis_index("row")
    col = lax.axis_index("col")
    layer = lax.axis_index("layer")
    place = jnp.stack([row, col, layer]).astype(jnp.int32)
    smem = pl.BlockSpec(memory_space=pltpu.SMEM)
    vmem = pl.BlockSpec(memory_space=pltpu.VMEM)
    anywhere = pl.BlockSpec(memory_space=pl.ANY)

    mine = lax.dynamic_slice_in_dim(x_blocks, layer * SPAN, SPAN, 0)
    mine = sent(mine, spread)
    masks = pl.pallas_call(
        mask_kernel,
        out_shape=jax.ShapeDtypeStruct((NX, NEAR, BS, LANES), jnp.bfloat16),
        in_specs=[smem, smem],
        out_specs=vmem,
        name="masks",
    )(place, shifts)
    near = sent(x_blocks, along_z(0))
    far = sent(x_blocks, along_z(1))
    mine = jnp.broadcast_to(mine[None], (NY, SPAN, BS, LANES))
    near, masks = lax.optimization_barrier((near, masks))
    left = lax.all_to_all(mine, "col", 0, 0)
    last = sent(near, along_z(1))
    twins = sent(jnp.concatenate([x_blocks, near], axis=0), other_core)
    twin_last = sent(jnp.concatenate([far, last], axis=0), other_core)
    parts = pl.pallas_call(
        product_kernel,
        out_shape=jax.ShapeDtypeStruct((NX, SPAN, BS, LANES), jnp.float32),
        in_specs=[smem, smem] + [vmem] * 2 + [anywhere] * 6,
        out_specs=vmem,
        scratch_shapes=[
            pltpu.VMEM((NEAR, RANGE, BS, LANES), jnp.bfloat16),
            pltpu.SemaphoreType.DMA((NEAR,)),
        ],
        compiler_params=pltpu.CompilerParams(vmem_limit_bytes=12 * 1024 * 1024),
        name="range_products",
    )(place, shifts, masks, left, x_blocks, near, far, last, twins, twin_last)
    return jnp.sum(swapped_along_x(parts), axis=0).astype(jnp.bfloat16)


def solution(mesh):
    return jax.shard_map(
        local,
        mesh=mesh,
        in_specs=(P("row", None, "col"), P()),
        out_specs=P(("row", "layer"), None, "col"),
        check_vma=False,
    )
```

```python
import jax
import jax.numpy as jnp
from jax import lax
from jax.experimental import pallas as pl
from jax.experimental.pallas import tpu as pltpu
from jax.sharding import PartitionSpec as P

AXES = ("row", "col", "layer")
NX, NZ, NY, NL = 4, 4, 8, 4
BS, RANGE, SPAN = 32, 64, 16
LANES = 128
NEAR = 8


def device_pairs(move):
    def index(x, z, core, y):
        return ((x * NZ + z % NZ) * 2 + core) * NY * NL + y * NL + z // NZ

    pairs = []
    for x in range(NX):
        for z in range(NZ * NL):
            for core in range(2):
                for y in range(NY):
                    tx, tz, tcore, ty = move(x, z, core, y)
                    pairs.append((index(x, z, core, y), index(tx % NX, tz % (NZ * NL), tcore, ty % NY)))
    return pairs


def sent(value, move):
    return lax.ppermute(value, AXES, device_pairs(move))


def other_core(x, z, core, y):
    return x, z, 1 - core, y


def along_z(turn):
    return lambda x, z, core, y: (x, z ^ (1 if core == turn else 3), core, y)


def spread(x, z, core, y):
    near_x, side = y // 2, y % 2
    turn = (x - near_x) % NX
    return near_x, z, core, (y + turn if side else y - turn)


def swapped_along_x(value):
    groups = [[x * NEAR + n for x in range(NX)] for n in range(NEAR)]
    return lax.all_to_all(value, "row", 0, 0, axis_index_groups=groups)


def mask_kernel(place_ref, shifts_ref, masks_ref):
    row = place_ref[0]
    col = place_ref[1]
    near = (row >> 3) * NEAR
    lane_block = lax.broadcasted_iota(jnp.int32, (BS, LANES), 1) // BS

    def mask_step(j, carry):
        source = near + j
        for t in range(NX):
            target = t * NEAR + (row & (NEAR - 1))
            value = jnp.zeros((BS, LANES), jnp.float32)
            for b in range(4):
                own_range = col * 4 + b
                total = shifts_ref[target, source] + shifts_ref[source, own_range]
                total = (total - shifts_ref[target, own_range]) & (RANGE - 1)
                value = jnp.where(lane_block == b, jnp.where(total == 0, 1.0, 0.0), value)
            masks_ref[t, j] = value.astype(jnp.bfloat16)
        return carry

    lax.fori_loop(0, NEAR, mask_step, 0)


def product_kernel(
    place_ref, shifts_ref, masks, left, pair, far, twin_pair, twin_far, out, right, sems
):
    row = place_ref[0]
    layer = place_ref[2]
    core = row & 1
    zl = (row >> 1) & 3
    x = row >> 3
    near = x * NEAR

    first = jnp.where(core == 0, 1, 3)
    second = jnp.where(core == 0, 3, 1)
    pieces = [(pair, 0, 0, core), (pair, 1, first, core), (far, 0, second, core), (far, 1, 2, core)]
    pieces += [(twin_pair, 0, 0, 1 - core), (twin_pair, 1, second, 1 - core)]
    pieces += [(twin_far, 0, first, 1 - core), (twin_far, 1, 2, 1 - core)]
    copies = []
    for n, (piece, half, turn, parity) in enumerate(pieces):
        slot = (zl ^ turn) * 2 + parity
        copies.append(pltpu.make_async_copy(piece.at[pl.ds(half * RANGE, RANGE)], right.at[slot], sems.at[n]))
    for copy in copies:
        copy.start()
    for copy in copies:
        copy.wait()

    def position_step(p, carry):
        place = layer * SPAN + p
        for t in range(NX):
            target = t * NEAR + (row & (NEAR - 1))
            turn = (t - x) & (NX - 1)
            low, high = (2 * x - turn) & (NY - 1), (2 * x + 1 + turn) & (NY - 1)
            lhs = jnp.concatenate([left[low, p], left[high, p]], axis=1)
            rows = []
            for j in range(NEAR):
                q = (place + shifts_ref[target, near + j]) & (RANGE - 1)
                rows.append(right[j, q] * masks[t, j])
            rhs = jnp.concatenate(rows, axis=0)
            out[t, p] = jnp.dot(lhs, rhs, preferred_element_type=jnp.float32)
        return carry

    lax.fori_loop(0, SPAN, position_step, 0, unroll=4)


def local(x_blocks, shifts):
    row = lax.axis_index("row")
    col = lax.axis_index("col")
    layer = lax.axis_index("layer")
    place = jnp.stack([row, col, layer]).astype(jnp.int32)
    smem = pl.BlockSpec(memory_space=pltpu.SMEM)
    vmem = pl.BlockSpec(memory_space=pltpu.VMEM)
    anywhere = pl.BlockSpec(memory_space=pl.ANY)

    mine = lax.dynamic_slice_in_dim(x_blocks, layer * SPAN, SPAN, 0)
    mine = sent(mine, spread)
    masks = pl.pallas_call(
        mask_kernel,
        out_shape=jax.ShapeDtypeStruct((NX, NEAR, BS, LANES), jnp.bfloat16),
        in_specs=[smem, smem],
        out_specs=vmem,
        name="masks",
    )(place, shifts)
    near = sent(x_blocks, along_z(0))
    near, masks, mine = lax.optimization_barrier((near, masks, mine))
    left = lax.all_to_all(jnp.broadcast_to(mine[None], (NY, SPAN, BS, LANES)), "col", 0, 0)
    pair = jnp.concatenate([x_blocks, near], axis=0)
    far = sent(pair, along_z(1))
    twin_pair = sent(pair, other_core)
    twin_far = sent(far, other_core)
    parts = pl.pallas_call(
        product_kernel,
        out_shape=jax.ShapeDtypeStruct((NX, SPAN, BS, LANES), jnp.float32),
        in_specs=[smem, smem] + [vmem] * 2 + [anywhere] * 4,
        out_specs=vmem,
        scratch_shapes=[
            pltpu.VMEM((NEAR, RANGE, BS, LANES), jnp.bfloat16),
            pltpu.SemaphoreType.DMA((NEAR,)),
        ],
        compiler_params=pltpu.CompilerParams(vmem_limit_bytes=12 * 1024 * 1024),
        name="range_products",
    )(place, shifts, masks, left, pair, far, twin_pair, twin_far)
    return jnp.sum(swapped_along_x(parts), axis=0).astype(jnp.bfloat16)


def solution(mesh):
    return jax.shard_map(
        local,
        mesh=mesh,
        in_specs=(P("row", None, "col"), P()),
        out_specs=P(("row", "layer"), None, "col"),
        check_vma=False,
    )
```
